32 devices in a mesh: dp: 4 (over y, core), cent: 8 (over z, x).
Axes of the slice: x: 2, y: 2, z: 4, core: 2. Of those that a mesh axis runs over, the one named last changes fastest.
Arguments:
- features: bfloat16 [4096, 1024], P('dp', 'cent'), may hold values from -128 to 128
- centroids: bfloat16 [16384, 1024], P('cent'), may hold values from -2 to 2
- row_weight: float32 [4096], P('dp'), may hold values from 0.5 to 18
- centroid_share: float32 [16384], P('cent'), may hold values from 0.5 to 18
Outputs:
- centroid_means: float32 [1024, 16384], P('dp', 'cent')
- centroid_mass: float32 [16384], P('cent')
The draws below stay inside these ranges and needn't reach their ends.
All inputs are finite; a program needn't handle non-finite values.
Results may differ from the reference program's by a relative error of at most 0.001.
The reference program's roundings to bfloat16 on the way (of `weights`) count: a program that leaves them out, or rounds other values in their place, can miss the bound.
Values may be sent and summed in bfloat16 or wider, within the bound.
A program may use at most 64 MiB of HBM per device.

```python
import math
import jax
import jax.numpy as jnp
from jax import lax

D = 1024
K_DEV = 2048
ITERS = 3
ROWS = 4096
CENTROIDS = 16384
N_CENT = 8


def shared_draw(key):
    key_cent = jax.random.fold_in(key, 101)
    key_feat = jax.random.fold_in(key, 202)
    spread = 2.0 / math.sqrt(D)
    centers = jnp.clip(jax.random.normal(key_cent, (CENTROIDS, D), jnp.float32), -6.0, 6.0) * spread
    centers = centers.astype(jnp.bfloat16).astype(jnp.float32)
    base = jnp.clip(jax.random.normal(jax.random.fold_in(key_feat, 1), (ROWS, D), jnp.float32), -6.0, 6.0)
    feats = base
    return (feats, centers)


def rising_draw(key, length):
    position = jnp.arange(length).astype(jnp.float32) / length
    factor = jnp.exp(jax.random.uniform(key, (length,), jnp.float32, math.log(0.5), math.log(2.0)))
    return factor * jnp.exp(position * math.log(3.0))


def draw_features(key, part):
    return shared_draw(key)[0].astype(jnp.bfloat16)


def draw_centroids(key, part):
    return shared_draw(key)[1].astype(jnp.bfloat16)


def draw_row_weight(key, part):
    return rising_draw(jax.random.fold_in(key, 303), ROWS)


def draw_centroid_share(key, part):
    return rising_draw(jax.random.fold_in(key, 404), CENTROIDS)


def setup_inputs(seed: int = 0) -> dict:
    streams_of = jax.random.split(jax.random.key(seed), 5)
    return {
        "features": draw_features(jax.random.fold_in(streams_of[4], 71), 0),
        "centroids": draw_centroids(jax.random.fold_in(streams_of[4], 71), 0),
        "row_weight": draw_row_weight(jax.random.fold_in(streams_of[4], 71), 0),
        "centroid_share": draw_centroid_share(jax.random.fold_in(streams_of[4], 71), 0),
    }


def reference(features, centroids, row_weight, centroid_share):
    feats = features.astype(jnp.float32)
    blocks = centroids.astype(jnp.float32).reshape(N_CENT, K_DEV, D)
    shares = centroid_share.reshape(N_CENT, K_DEV)

    def scores_of(block):
        return jnp.dot(feats, block.T, precision=lax.Precision.HIGHEST)

    row_max = jnp.max(lax.map(lambda block: jnp.max(scores_of(block), axis=1), blocks), axis=0)

    def kernel_of(block):
        return jnp.exp(scores_of(block) - row_max[:, None])

    def row_step(column_scale):
        def accumulate(running, pair):
            block, scale_part = pair
            return running + jnp.sum(kernel_of(block) * scale_part[None, :], axis=1), None

        running, unused = lax.scan(accumulate, jnp.zeros((ROWS,), jnp.float32), (blocks, column_scale))
        return row_weight / running

    def column_step(row_scale):
        def one_block(pair):
            block, share_part = pair
            return share_part / jnp.sum(kernel_of(block) * row_scale[:, None], axis=0)

        return lax.map(one_block, (blocks, shares))

    column_scale = jnp.ones((N_CENT, K_DEV), jnp.float32)
    for iteration in range(ITERS):
        row_scale = row_step(column_scale)
        column_scale = column_step(row_scale)
    row_scale = row_step(column_scale)

    def finish(pair):
        block, scale_part = pair
        transport = kernel_of(block) * row_scale[:, None] * scale_part[None, :]
        centroid_total = jnp.sum(transport, axis=0)
        weights = lax.optimization_barrier(transport.astype(jnp.bfloat16)).astype(jnp.float32)
        weighted = jnp.dot(feats.T, weights, precision=lax.Precision.HIGHEST)
        return weighted / centroid_total[None, :], centroid_total

    means_blocks, mass_blocks = lax.map(finish, (blocks, column_scale))
    centroid_means = jnp.transpose(means_blocks, (1, 0, 2)).reshape(D, CENTROIDS)
    return centroid_means, mass_blocks.reshape(CENTROIDS)
```

```python
import functools

import jax
import jax.numpy as jnp
from jax import lax
from jax.experimental import pallas as pl
from jax.experimental.pallas import tpu as pltpu
from jax.sharding import PartitionSpec as P

ITERS = 3
LANES = 128
MESH = pl.DeviceIdType.MESH


def kernel_body(
    nc, nd, nx, nq,
    ft_in, cent_ref, rw_ref, share_ref,
    means_ref, mass_ref,
    ft, kt, wt, xs0, xr0, xs, xr, ys, yr, p1, r1, s2, r2,
    f_send, f_recv, x0_send, x0_recv, x_send, x_recv, y_send, y_recv,
    p1_send, p1_recv, s2_send, s2_recv,
):
    nz = nc // nx
    ny = nd // 2
    me = lax.axis_index("cent")
    md = lax.axis_index("dp")
    z, x = me // nx, me % nx
    y, core = md // 2, md % 2
    dloc, rows = ft_in.shape
    kc = cent_ref.shape[0]
    ds = means_ref.shape[0]
    tiles = rows // LANES
    chunks = kc // LANES
    kq = kc // nq

    barrier = pltpu.get_barrier_semaphore()
    for d in range(1, nc):
        pl.semaphore_signal(barrier, inc=1, device_id={"cent": (me + d) % nc}, device_id_type=MESH)
    for d in range(1, nd):
        pl.semaphore_signal(barrier, inc=1, device_id={"dp": (md + d) % nd}, device_id_type=MESH)
    pl.semaphore_wait(barrier, nc + nd - 2)

    pending = []

    def remote(src, dst, send, recv, target):
        copy = pltpu.make_async_remote_copy(
            src_ref=src, dst_ref=dst, send_sem=send, recv_sem=recv,
            device_id=target, device_id_type=MESH,
        )
        copy.start()
        pending.append(copy)
        return copy

    def slab(j):
        return pl.ds(pl.multiple_of(j * dloc, dloc), dloc)

    inbound = {}
    for dx in range(1, nx):
        target = z * nx + (x + dx) % nx
        inbound[dx] = remote(ft_in, ft.at[slab(me)], f_send.at[dx], f_recv.at[dx], {"cent": target})
    for dz in range(1, nz):
        target = ((z + dz) % nz) * nx + x
        k = dz * nx
        inbound[k] = remote(ft_in, ft.at[slab(me)], f_send.at[k], f_recv.at[k], {"cent": target})
    ft[slab(me), :] = ft_in[...]
    order = sorted(range(1, nz), key=lambda d: min(d, nz - d))
    for dz in order:
        inbound[dz * nx].wait_recv()
        block = ((z + nz - dz) % nz) * nx + x
        for dx in range(1, nx):
            k = dz * nx + dx
            target = z * nx + (x + dx) % nx
            inbound[k] = remote(
                ft.at[slab(block)], ft.at[slab(block)], f_send.at[k], f_recv.at[k], {"cent": target}
            )
    for k in range(1, nc):
        if k % nx or k < nx:
            inbound[k].wait_recv()

    def exchange(axis, n, mine, source, buffer, send, recv):
        buffer[pl.ds(mine, 1)] = source[...][None]
        copies = [
            remote(source, buffer.at[mine], send.at[d], recv.at[d], {axis: (mine + d) % n})
            for d in range(1, n)
        ]
        for copy in copies:
            copy.wait_recv()
        return buffer[...]

    def chunk(i):
        return pl.ds(pl.multiple_of(i * LANES, LANES), LANES)

    def lane(t):
        return slice(t * LANES, (t + 1) * LANES)

    def fold(block):
        return jnp.sum(block.reshape(LANES // 8, 8, LANES), axis=0)

    def row_vector(parts):
        return jnp.concatenate([jnp.sum(p, axis=0, keepdims=True) for p in parts], axis=1)

    step = 2 * LANES

    def score(i, peak):
        at = pl.ds(pl.multiple_of(i * step, step), step)
        s = jnp.dot(cent_ref[at, :], ft[...], preferred_element_type=jnp.float32)
        kt[at, :] = s
        return jnp.maximum(peak, jnp.max(s.reshape(step // 8, 8, rows), axis=0))

    peak = lax.fori_loop(0, kc // step, score, jnp.full((8, rows), -jnp.inf, jnp.float32))
    peak = jnp.max(peak, axis=0, keepdims=True)

    zeros = tuple(jnp.zeros((8, LANES), jnp.float32) for t in range(tiles))

    def exponent(i, parts):
        out = []
        for t in range(tiles):
            e = jnp.exp(kt[chunk(i), lane(t)] - peak[:, lane(t)])
            kt[chunk(i), lane(t)] = e
            out.append(parts[t] + fold(e))
        return tuple(out)

    local = row_vector(lax.fori_loop(0, chunks, exponent, zeros))
    xs0[0:1, :] = peak
    xs0[1:2, :] = local
    both = exchange("cent", nc, me, xs0, xr0, x0_send, x0_recv)
    top = jnp.max(both[:, 0, :], axis=0, keepdims=True)
    total = jnp.sum(both[:, 1, :] * jnp.exp(both[:, 0, :] - top), axis=0, keepdims=True)
    shift = jnp.exp(peak - top)
    weight = rw_ref[...]
    row_scale = weight / total * shift

    def columns(row_scale, k):
        def one(i, carry):
            acc = kt[chunk(i), lane(0)] * row_scale[:, lane(0)]
            for t in range(1, tiles):
                acc = acc + kt[chunk(i), lane(t)] * row_scale[:, lane(t)]
            ys[k, :, chunk(i)] = jnp.sum(acc.T, axis=0, keepdims=True)
            return carry

        lax.fori_loop(0, chunks, one, 0)
        sums = exchange("dp", nd, md, ys.at[k], yr.at[k], y_send.at[k], y_recv.at[k])
        return jnp.sum(sums, axis=0)

    def down(ref, i):
        return jnp.broadcast_to(ref[:, chunk(i)], (LANES, LANES)).T

    for k in range(ITERS):
        mass_ref[...] = share_ref[...] / columns(row_scale, k)

        def one(i, parts):
            scale = down(mass_ref, i)
            return tuple(parts[t] + fold(kt[chunk(i), lane(t)] * scale) for t in range(tiles))

        xs[k] = row_vector(lax.fori_loop(0, chunks, one, zeros)) * shift
        sums = exchange("cent", nc, me, xs.at[k], xr.at[k], x_send.at[k], x_recv.at[k])
        row_scale = weight / jnp.sum(sums, axis=0) * shift

    def transport(i, carry):
        scale = down(mass_ref, i)
        acc = jnp.zeros((LANES, LANES), jnp.float32)
        for t in range(tiles):
            v = kt[chunk(i), lane(t)] * row_scale[:, lane(t)] * scale
            wt[chunk(i), lane(t)] = v.astype(jnp.bfloat16)
            acc = acc + v
        ys[ITERS, :, chunk(i)] = jnp.sum(acc.T, axis=0, keepdims=True)
        return carry

    lax.fori_loop(0, chunks, transport, 0)
    yr[ITERS, pl.ds(md, 1)] = ys[ITERS][None]
    mass_copies = [
        remote(
            ys.at[ITERS], yr.at[ITERS, md], y_send.at[ITERS, d], y_recv.at[ITERS, d],
            {"dp": (md + d) % nd},
        )
        for d in range(1, nd)
    ]

    def partial(owner, q):
        at = pl.ds(pl.multiple_of(owner * ds, ds), ds)
        return lax.dot_general(
            ft[at, :], wt[q * kq:(q + 1) * kq, :], (((1,), (1,)), ((), ())),
            preferred_element_type=jnp.float32,
        )

    pair = y * 2 + (1 - core)
    first = {}

    def to_core(dy, q):
        p1[dy, q] = partial(((y + dy) % ny) * 2 + (1 - core), q)
        first[dy, q] = remote(
            p1.at[dy, q], r1.at[dy, q], p1_send.at[dy, q], p1_recv.at[dy, q], {"dp": pair}
        )

    second = {}

    def along_y(dy, q):
        owner = ((y + dy) % ny) * 2 + core
        mine = partial(owner, q)
        first[dy, q].wait_recv()
        s2[dy - 1, q] = mine + r1[dy, q]
        second[dy, q] = remote(
            s2.at[dy - 1, q], r2.at[dy - 1, q],
            s2_send.at[dy - 1, q], s2_recv.at[dy - 1, q], {"dp": owner},
        )

    todo = [(dy, q) for q in range(nq) for dy in range(1, ny)]
    to_core(*todo[0])
    for i, item in enumerate(todo):
        if i + 1 < len(todo):
            to_core(*todo[i + 1])
        along_y(*item)
    for q in range(nq):
        to_core(0, q)
    for copy in mass_copies:
        copy.wait_recv()
    mass = jnp.sum(yr[ITERS], axis=0)
    mass_ref[...] = mass
    for q in range(nq):
        mine = partial(md, q)
        first[0, q].wait_recv()
        means_ref[:, q * kq:(q + 1) * kq] = mine + r1[0, q]
    for q in range(nq):
        at = slice(q * kq, (q + 1) * kq)
        value = means_ref[:, at]
        for dy in range(1, ny):
            second[dy, q].wait_recv()
            value = value + r2[dy - 1, q]
        means_ref[:, at] = value / mass[:, at]

    for copy in pending:
        copy.wait_send()


def solution(mesh):
    nc, nd = mesh.shape["cent"], mesh.shape["dp"]
    ny = nd // 2
    nx = ny if nc % ny == 0 else 1
    nq = 8

    def per_device(features, centroids, row_weight, centroid_share):
        rows, dloc = features.shape
        kc, width = centroids.shape
        ds = width // nd
        f32, bf16 = jnp.float32, jnp.bfloat16
        dma = pltpu.SemaphoreType.DMA
        vmem = pl.BlockSpec(memory_space=pltpu.VMEM)
        means, mass = pl.pallas_call(
            functools.partial(kernel_body, nc, nd, nx, nq),
            out_shape=(
                jax.ShapeDtypeStruct((ds, kc), f32),
                jax.ShapeDtypeStruct((1, kc), f32),
            ),
            in_specs=[vmem] * 4,
            out_specs=(vmem, vmem),
            scratch_shapes=[
                pltpu.VMEM((width, rows), bf16),
                pltpu.VMEM((kc, rows), f32),
                pltpu.VMEM((kc, rows), bf16),
                pltpu.VMEM((2, rows), f32),
                pltpu.VMEM((nc, 2, rows), f32),
                pltpu.VMEM((ITERS, 1, rows), f32),
                pltpu.VMEM((ITERS, nc, 1, rows), f32),
                pltpu.VMEM((ITERS + 1, 1, kc), f32),
                pltpu.VMEM((ITERS + 1, nd, 1, kc), f32),
                pltpu.VMEM((ny, nq, ds, kc // nq), f32),
                pltpu.VMEM((ny, nq, ds, kc // nq), f32),
                pltpu.VMEM((ny - 1, nq, ds, kc // nq), f32),
                pltpu.VMEM((ny - 1, nq, ds, kc // nq), f32),
                dma((nc,)), dma((nc,)),
                dma((nc,)), dma((nc,)),
                dma((ITERS, nc)), dma((ITERS, nc)),
                dma((ITERS + 1, nd)), dma((ITERS + 1, nd)),
                dma((ny, nq)), dma((ny, nq)),
                dma((ny - 1, nq)), dma((ny - 1, nq)),
            ],
            compiler_params=pltpu.CompilerParams(
                collective_id=0, has_side_effects=True, vmem_limit_bytes=50 * 1024 * 1024
            ),
        )(features.T, centroids, row_weight[None], centroid_share[None])
        return means, mass[0]

    in_specs = (P("dp", "cent"), P("cent", None), P("dp"), P("cent"))
    out_specs = (P("dp", "cent"), P("cent"))
    return jax.shard_map(
        per_device, mesh=mesh, in_specs=in_specs, out_specs=out_specs, check_vma=False
    )
```

```python
import functools

import jax
import jax.numpy as jnp
from jax import lax
from jax.experimental import pallas as pl
from jax.experimental.pallas import tpu as pltpu
from jax.sharding import PartitionSpec as P

ITERS = 3
LANES = 128
MESH = pl.DeviceIdType.MESH


def kernel_body(
    nc, nd, nx, nq,
    ft_in, cent_ref, rw_ref, share_ref,
    means_ref, mass_ref,
    cent, load_sem, ft, kt, wt, xs0, xr0, xs, xr, ys, yr, p1, r1, s2, r2,
    f_send, f_recv, x0_send, x0_recv, x_send, x_recv, y_send, y_recv,
    p1_send, p1_recv, s2_send, s2_recv,
):
    nz = nc // nx
    ny = nd // 2
    me = lax.axis_index("cent")
    md = lax.axis_index("dp")
    z, x = me // nx, me % nx
    y, core = md // 2, md % 2
    dloc, rows = ft_in.shape
    kc = cent_ref.shape[0]
    ds = means_ref.shape[0]
    tiles = rows // LANES
    chunks = kc // LANES
    kq = kc // nq

    barrier = pltpu.get_barrier_semaphore()
    for d in range(1, nc):
        pl.semaphore_signal(barrier, inc=1, device_id={"cent": (me + d) % nc}, device_id_type=MESH)
    for d in range(1, nd):
        pl.semaphore_signal(barrier, inc=1, device_id={"dp": (md + d) % nd}, device_id_type=MESH)
    pl.semaphore_wait(barrier, nc + nd - 2)

    pending = []

    def remote(src, dst, send, recv, target):
        copy = pltpu.make_async_remote_copy(
            src_ref=src, dst_ref=dst, send_sem=send, recv_sem=recv,
            device_id=target, device_id_type=MESH,
        )
        copy.start()
        pending.append(copy)
        return copy

    def slab(j):
        return pl.ds(pl.multiple_of(j * dloc, dloc), dloc)

    load = pltpu.make_async_copy(cent_ref, cent, load_sem)
    load.start()

    half = dloc // 2
    inbound = {}

    def send(source, block, k, piece, target):
        at = pl.ds(pl.multiple_of(block * dloc + piece * half, half), half)
        inbound[k, piece] = remote(
            ft.at[at] if source is None else source.at[piece * half:(piece + 1) * half],
            ft.at[at], f_send.at[k, piece], f_recv.at[k, piece], {"cent": target},
        )

    up = ((z + 1) % nz) * nx + x
    low = ((z + nz - 1) % nz) * nx + x
    ups, downs = nz // 2, (nz - 1) // 2
    for piece in range(2):
        if ups:
            send(ft_in, me, nx, piece, up)
        if downs:
            send(ft_in, me, (nz - 1) * nx, piece, low)
        for dx in range(1, nx):
            send(ft_in, me, dx, piece, z * nx + (x + dx) % nx)
    ft[slab(me), :] = ft_in[...]
    seen = [0]
    for hop in range(1, ups + 1):
        here = [(hop, up, ups)] + ([(nz - hop, low, downs)] if hop <= downs else [])
        for piece in range(2):
            for dz, onward, most in here:
                inbound[dz * nx, piece].wait_recv()
                block = ((z + nz - dz) % nz) * nx + x
                if hop < most:
                    ahead = dz + 1 if onward is up else dz - 1
                    send(None, block, ahead * nx, piece, onward)
                for dx in range(1, nx):
                    send(None, block, dz * nx + dx, piece, z * nx + (x + dx) % nx)
        seen += [dz for dz, onward, most in here]

    def exchange(axis, n, mine, source, buffer, send, recv):
        buffer[pl.ds(mine, 1)] = source[...][None]
        copies = [
            remote(source, buffer.at[mine], send.at[d], recv.at[d], {axis: (mine + d) % n})
            for d in range(1, n)
        ]
        for copy in copies:
            copy.wait_recv()
        return buffer[...]

    def chunk(i):
        return pl.ds(pl.multiple_of(i * LANES, LANES), LANES)

    def lane(t):
        return slice(t * LANES, (t + 1) * LANES)

    def fold(block):
        return jnp.sum(block.reshape(LANES // 8, 8, LANES), axis=0)

    def row_vector(parts):
        return jnp.concatenate([jnp.sum(p, axis=0, keepdims=True) for p in parts], axis=1)

    load.wait()
    step = 2 * LANES
    group = nx * dloc
    peak = jnp.full((8, rows), -jnp.inf, jnp.float32)
    for n, dz in enumerate(seen):
        for dx in range(1, nx):
            for piece in range(2):
                inbound[dz * nx + dx, piece].wait_recv()
        across = pl.ds(pl.multiple_of(((z + nz - dz) % nz) * group, group), group)

        def score(i, peak, n=n, across=across):
            at = pl.ds(pl.multiple_of(i * step, step), step)
            s = jnp.dot(cent[at, across], ft[across, :], preferred_element_type=jnp.float32)
            if n:
                s = s + kt[at, :]
            kt[at, :] = s
            if n < nz - 1:
                return peak
            return jnp.maximum(peak, jnp.max(s.reshape(step // 8, 8, rows), axis=0))

        peak = lax.fori_loop(0, kc // step, score, peak)
    peak = jnp.max(peak, axis=0, keepdims=True)

    zeros = tuple(jnp.zeros((8, LANES), jnp.float32) for t in range(tiles))

    def exponent(i, parts):
        out = []
        for t in range(tiles):
            e = jnp.exp(kt[chunk(i), lane(t)] - peak[:, lane(t)])
            kt[chunk(i), lane(t)] = e
            out.append(parts[t] + fold(e))
        return tuple(out)

    local = row_vector(lax.fori_loop(0, chunks, exponent, zeros))
    xs0[0:1, :] = peak
    xs0[1:2, :] = local
    both = exchange("cent", nc, me, xs0, xr0, x0_send, x0_recv)
    top = jnp.max(both[:, 0, :], axis=0, keepdims=True)
    total = jnp.sum(both[:, 1, :] * jnp.exp(both[:, 0, :] - top), axis=0, keepdims=True)
    shift = jnp.exp(peak - top)
    weight = rw_ref[...]
    row_scale = weight / total * shift

    def columns(row_scale, k):
        def one(i, carry):
            acc = kt[chunk(i), lane(0)] * row_scale[:, lane(0)]
            for t in range(1, tiles):
                acc = acc + kt[chunk(i), lane(t)] * row_scale[:, lane(t)]
            ys[k, :, chunk(i)] = jnp.sum(acc.T, axis=0, keepdims=True)
            return carry

        lax.fori_loop(0, chunks, one, 0)
        sums = exchange("dp", nd, md, ys.at[k], yr.at[k], y_send.at[k], y_recv.at[k])
        return jnp.sum(sums, axis=0)

    def down(ref, i):
        return jnp.broadcast_to(ref[:, chunk(i)], (LANES, LANES)).T

    for k in range(ITERS):
        mass_ref[...] = share_ref[...] / columns(row_scale, k)

        def one(i, parts):
            scale = down(mass_ref, i)
            return tuple(parts[t] + fold(kt[chunk(i), lane(t)] * scale) for t in range(tiles))

        xs[k] = row_vector(lax.fori_loop(0, chunks, one, zeros)) * shift
        sums = exchange("cent", nc, me, xs.at[k], xr.at[k], x_send.at[k], x_recv.at[k])
        row_scale = weight / jnp.sum(sums, axis=0) * shift

    def transport(i, carry):
        scale = down(mass_ref, i)
        acc = jnp.zeros((LANES, LANES), jnp.float32)
        for t in range(tiles):
            v = kt[chunk(i), lane(t)] * row_scale[:, lane(t)] * scale
            wt[chunk(i), lane(t)] = v.astype(jnp.bfloat16)
            acc = acc + v
        ys[ITERS, :, chunk(i)] = jnp.sum(acc.T, axis=0, keepdims=True)
        return carry

    lax.fori_loop(0, chunks, transport, 0)
    yr[ITERS, pl.ds(md, 1)] = ys[ITERS][None]
    mass_copies = [
        remote(
            ys.at[ITERS], yr.at[ITERS, md], y_send.at[ITERS, d], y_recv.at[ITERS, d],
            {"dp": (md + d) % nd},
        )
        for d in range(1, nd)
    ]

    def partial(owner, q):
        at = pl.ds(pl.multiple_of(owner * ds, ds), ds)
        return lax.dot_general(
            ft[at, :], wt[q * kq:(q + 1) * kq, :], (((1,), (1,)), ((), ())),
            preferred_element_type=jnp.float32,
        )

    pair = y * 2 + (1 - core)
    first = {}

    def to_core(dy, q):
        p1[dy, q] = partial(((y + dy) % ny) * 2 + (1 - core), q)
        first[dy, q] = remote(
            p1.at[dy, q], r1.at[dy, q], p1_send.at[dy, q], p1_recv.at[dy, q], {"dp": pair}
        )

    second = {}

    def along_y(dy, q):
        owner = ((y + dy) % ny) * 2 + core
        mine = partial(owner, q)
        first[dy, q].wait_recv()
        s2[dy - 1, q] = mine + r1[dy, q]
        second[dy, q] = remote(
            s2.at[dy - 1, q], r2.at[dy - 1, q],
            s2_send.at[dy - 1, q], s2_recv.at[dy - 1, q], {"dp": owner},
        )

    todo = [(dy, q) for q in range(nq) for dy in range(1, ny)]
    to_core(*todo[0])
    for i, item in enumerate(todo):
        if i + 1 < len(todo):
            to_core(*todo[i + 1])
        along_y(*item)
    for q in range(nq):
        to_core(0, q)
    for copy in mass_copies:
        copy.wait_recv()
    mass = jnp.sum(yr[ITERS], axis=0)
    mass_ref[...] = mass
    for q in range(nq):
        mine = partial(md, q)
        first[0, q].wait_recv()
        means_ref[:, q * kq:(q + 1) * kq] = mine + r1[0, q]
    for q in range(nq):
        at = slice(q * kq, (q + 1) * kq)
        value = means_ref[:, at]
        for dy in range(1, ny):
            second[dy, q].wait_recv()
            value = value + r2[dy - 1, q]
        means_ref[:, at] = value / mass[:, at]

    for copy in pending:
        copy.wait_send()


def solution(mesh):
    nc, nd = mesh.shape["cent"], mesh.shape["dp"]
    ny = nd // 2
    nx = ny if nc % ny == 0 else 1
    nq = 8

    def per_device(features, centroids, row_weight, centroid_share):
        rows, dloc = features.shape
        kc, width = centroids.shape
        ds = width // nd
        f32, bf16 = jnp.float32, jnp.bfloat16
        dma = pltpu.SemaphoreType.DMA
        vmem = pl.BlockSpec(memory_space=pltpu.VMEM)
        means, mass = pl.pallas_call(
            functools.partial(kernel_body, nc, nd, nx, nq),
            out_shape=(
                jax.ShapeDtypeStruct((ds, kc), f32),
                jax.ShapeDtypeStruct((1, kc), f32),
            ),
            in_specs=[vmem, pl.BlockSpec(memory_space=pl.ANY), vmem, vmem],
            out_specs=(vmem, vmem),
            scratch_shapes=[
                pltpu.VMEM((kc, width), bf16),
                dma(()),
                pltpu.VMEM((width, rows), bf16),
                pltpu.VMEM((kc, rows), f32),
                pltpu.VMEM((kc, rows), bf16),
                pltpu.VMEM((2, rows), f32),
                pltpu.VMEM((nc, 2, rows), f32),
                pltpu.VMEM((ITERS, 1, rows), f32),
                pltpu.VMEM((ITERS, nc, 1, rows), f32),
                pltpu.VMEM((ITERS + 1, 1, kc), f32),
                pltpu.VMEM((ITERS + 1, nd, 1, kc), f32),
                pltpu.VMEM((ny, nq, ds, kc // nq), f32),
                pltpu.VMEM((ny, nq, ds, kc // nq), f32),
                pltpu.VMEM((ny - 1, nq, ds, kc // nq), f32),
                pltpu.VMEM((ny - 1, nq, ds, kc // nq), f32),
                dma((nc, 2)), dma((nc, 2)),
                dma((nc,)), dma((nc,)),
                dma((ITERS, nc)), dma((ITERS, nc)),
                dma((ITERS + 1, nd)), dma((ITERS + 1, nd)),
                dma((ny, nq)), dma((ny, nq)),
                dma((ny - 1, nq)), dma((ny - 1, nq)),
            ],
            compiler_params=pltpu.CompilerParams(
                collective_id=0, has_side_effects=True, vmem_limit_bytes=50 * 1024 * 1024
            ),
        )(features.T, centroids, row_weight[None], centroid_share[None])
        return means, mass[0]

    in_specs = (P("dp", "cent"), P("cent", None), P("dp"), P("cent"))
    out_specs = (P("dp", "cent"), P("cent"))
    return jax.shard_map(
        per_device, mesh=mesh, in_specs=in_specs, out_specs=out_specs, check_vma=False
    )
```

```python
import functools

import jax
import jax.numpy as jnp
from jax import lax
from jax.experimental import pallas as pl
from jax.experimental.pallas import tpu as pltpu
from jax.sharding import PartitionSpec as P

ITERS = 3
LANES = 128
MESH = pl.DeviceIdType.MESH


def kernel_body(
    nc, nd, nx, nq,
    ft_in, cent_ref, rw_ref, share_ref,
    means_ref, mass_ref,
    cent, load_sem, ft, kt, wt, xs0, xr0, xs, xr, ys, yr, p1, r1, s2, r2, s2n, r2n,
    f_send, f_recv, x0_send, x0_recv, x_send, x_recv, y_send, y_recv,
    p1_send, p1_recv, s2_send, s2_recv,
):
    nz = nc // nx
    ny = nd // 2
    me = lax.axis_index("cent")
    md = lax.axis_index("dp")
    z, x = me // nx, me % nx
    y, core = md // 2, md % 2
    dloc, rows = ft_in.shape
    kc = cent_ref.shape[0]
    ds = means_ref.shape[0]
    tiles = rows // LANES
    chunks = kc // LANES
    kq = kc // nq

    barrier = pltpu.get_barrier_semaphore()
    for d in range(1, nc):
        pl.semaphore_signal(barrier, inc=1, device_id={"cent": (me + d) % nc}, device_id_type=MESH)
    for d in range(1, nd):
        pl.semaphore_signal(barrier, inc=1, device_id={"dp": (md + d) % nd}, device_id_type=MESH)
    pl.semaphore_wait(barrier, nc + nd - 2)

    pending = []

    def remote(src, dst, send, recv, target):
        copy = pltpu.make_async_remote_copy(
            src_ref=src, dst_ref=dst, send_sem=send, recv_sem=recv,
            device_id=target, device_id_type=MESH,
        )
        copy.start()
        pending.append(copy)
        return copy

    def slab(j):
        return pl.ds(pl.multiple_of(j * dloc, dloc), dloc)

    load = pltpu.make_async_copy(cent_ref, cent, load_sem)
    load.start()

    half = dloc // 2
    inbound = {}

    def send(source, block, k, piece, target):
        at = pl.ds(pl.multiple_of(block * dloc + piece * half, half), half)
        inbound[k, piece] = remote(
            ft.at[at] if source is None else source.at[piece * half:(piece + 1) * half],
            ft.at[at], f_send.at[k, piece], f_recv.at[k, piece], {"cent": target},
        )

    up = ((z + 1) % nz) * nx + x
    low = ((z + nz - 1) % nz) * nx + x
    ups, downs = nz // 2, (nz - 1) // 2
    for piece in range(2):
        if ups:
            send(ft_in, me, nx, piece, up)
        if downs:
            send(ft_in, me, (nz - 1) * nx, piece, low)
        for dx in range(1, nx):
            send(ft_in, me, dx, piece, z * nx + (x + dx) % nx)
    ft[slab(me), :] = ft_in[...]
    seen = [0]
    for hop in range(1, ups + 1):
        here = [(hop, up, ups)] + ([(nz - hop, low, downs)] if hop <= downs else [])
        for piece in range(2):
            for dz, onward, most in here:
                inbound[dz * nx, piece].wait_recv()
                block = ((z + nz - dz) % nz) * nx + x
                if hop < most:
                    ahead = dz + 1 if onward is up else dz - 1
                    send(None, block, ahead * nx, piece, onward)
                for dx in range(1, nx):
                    send(None, block, dz * nx + dx, piece, z * nx + (x + dx) % nx)
        seen += [dz for dz, onward, most in here]

    def exchange(axis, n, mine, source, buffer, send, recv):
        buffer[pl.ds(mine, 1)] = source[...][None]
        copies = [
            remote(source, buffer.at[mine], send.at[d], recv.at[d], {axis: (mine + d) % n})
            for d in range(1, n)
        ]
        for copy in copies:
            copy.wait_recv()
        return buffer[...]

    def chunk(i):
        return pl.ds(pl.multiple_of(i * LANES, LANES), LANES)

    def lane(t):
        return slice(t * LANES, (t + 1) * LANES)

    def fold(block):
        return jnp.sum(block.reshape(LANES // 8, 8, LANES), axis=0)

    def row_vector(parts):
        return jnp.concatenate([jnp.sum(p, axis=0, keepdims=True) for p in parts], axis=1)

    load.wait()
    step = 2 * LANES
    group = nx * dloc
    peak = jnp.full((8, rows), -jnp.inf, jnp.float32)
    for n, dz in enumerate(seen):
        for dx in range(1, nx):
            for piece in range(2):
                inbound[dz * nx + dx, piece].wait_recv()
        across = pl.ds(pl.multiple_of(((z + nz - dz) % nz) * group, group), group)

        def score(i, peak, n=n, across=across):
            at = pl.ds(pl.multiple_of(i * step, step), step)
            s = jnp.dot(cent[at, across], ft[across, :], preferred_element_type=jnp.float32)
            if n:
                s = s + kt[at, :]
            kt[at, :] = s
            if n < nz - 1:
                return peak
            return jnp.maximum(peak, jnp.max(s.reshape(step // 8, 8, rows), axis=0))

        peak = lax.fori_loop(0, kc // step, score, peak)
    peak = jnp.max(peak, axis=0, keepdims=True)

    zeros = tuple(jnp.zeros((8, LANES), jnp.float32) for t in range(tiles))

    def exponent(i, parts):
        out = []
        for t in range(tiles):
            e = jnp.exp(kt[chunk(i), lane(t)] - peak[:, lane(t)])
            kt[chunk(i), lane(t)] = e
            out.append(parts[t] + fold(e))
        return tuple(out)

    local = row_vector(lax.fori_loop(0, chunks, exponent, zeros))
    xs0[0:1, :] = peak
    xs0[1:2, :] = local
    both = exchange("cent", nc, me, xs0, xr0, x0_send, x0_recv)
    top = jnp.max(both[:, 0, :], axis=0, keepdims=True)
    total = jnp.sum(both[:, 1, :] * jnp.exp(both[:, 0, :] - top), axis=0, keepdims=True)
    shift = jnp.exp(peak - top)
    weight = rw_ref[...]
    row_scale = weight / total * shift

    def columns(row_scale, k):
        def one(i, carry):
            acc = kt[chunk(i), lane(0)] * row_scale[:, lane(0)]
            for t in range(1, tiles):
                acc = acc + kt[chunk(i), lane(t)] * row_scale[:, lane(t)]
            ys[k, :, chunk(i)] = jnp.sum(acc.T, axis=0, keepdims=True)
            return carry

        lax.fori_loop(0, chunks, one, 0)
        sums = exchange("dp", nd, md, ys.at[k], yr.at[k], y_send.at[k], y_recv.at[k])
        return jnp.sum(sums, axis=0)

    def down(ref, i):
        return jnp.broadcast_to(ref[:, chunk(i)], (LANES, LANES)).T

    for k in range(ITERS):
        mass_ref[...] = share_ref[...] / columns(row_scale, k)

        def one(i, parts):
            scale = down(mass_ref, i)
            return tuple(parts[t] + fold(kt[chunk(i), lane(t)] * scale) for t in range(tiles))

        xs[k] = row_vector(lax.fori_loop(0, chunks, one, zeros)) * shift
        sums = exchange("cent", nc, me, xs.at[k], xr.at[k], x_send.at[k], x_recv.at[k])
        row_scale = weight / jnp.sum(sums, axis=0) * shift

    def transport(i, carry):
        scale = down(mass_ref, i)
        acc = jnp.zeros((LANES, LANES), jnp.float32)
        for t in range(tiles):
            v = kt[chunk(i), lane(t)] * row_scale[:, lane(t)] * scale
            wt[chunk(i), lane(t)] = v.astype(jnp.bfloat16)
            acc = acc + v
        ys[ITERS, :, chunk(i)] = jnp.sum(acc.T, axis=0, keepdims=True)
        return carry

    lax.fori_loop(0, chunks, transport, 0)
    yr[ITERS, pl.ds(md, 1)] = ys[ITERS][None]
    mass_copies = [
        remote(
            ys.at[ITERS], yr.at[ITERS, md], y_send.at[ITERS, d], y_recv.at[ITERS, d],
            {"dp": (md + d) % nd},
        )
        for d in range(1, nd)
    ]

    def partial(owner, q):
        at = pl.ds(pl.multiple_of(owner * ds, ds), ds)
        return lax.dot_general(
            ft[at, :], wt[q * kq:(q + 1) * kq, :], (((1,), (1,)), ((), ())),
            preferred_element_type=jnp.float32,
        )

    pair = y * 2 + (1 - core)
    first = {}

    def to_core(dy, q):
        p1[dy, q] = partial(((y + dy) % ny) * 2 + (1 - core), q)
        first[dy, q] = remote(
            p1.at[dy, q], r1.at[dy, q], p1_send.at[dy, q], p1_recv.at[dy, q], {"dp": pair}
        )

    second = {}
    wide = s2.shape[1]

    def outgoing(q):
        return (s2, q) if q < wide else (s2n, q - wide)

    def incoming(q):
        return (r2, q) if q < wide else (r2n, q - wide)

    def along_y(dy, q):
        owner = ((y + dy) % ny) * 2 + core
        mine = partial(owner, q)
        first[dy, q].wait_recv()
        out, slot = outgoing(q)
        out[dy - 1, slot] = (mine + r1[dy, q]).astype(out.dtype)
        arriving, slot = incoming(q)
        second[dy, q] = remote(
            out.at[dy - 1, slot], arriving.at[dy - 1, slot],
            s2_send.at[dy - 1, q], s2_recv.at[dy - 1, q], {"dp": owner},
        )

    todo = [(dy, q) for q in range(nq) for dy in range(1, ny)]
    to_core(*todo[0])
    for i, item in enumerate(todo):
        if i + 1 < len(todo):
            to_core(*todo[i + 1])
        along_y(*item)
    for q in range(nq):
        to_core(0, q)
    for copy in mass_copies:
        copy.wait_recv()
    mass = jnp.sum(yr[ITERS], axis=0)
    mass_ref[...] = mass
    for q in range(nq):
        mine = partial(md, q)
        first[0, q].wait_recv()
        means_ref[:, q * kq:(q + 1) * kq] = mine + r1[0, q]
    for q in range(nq):
        at = slice(q * kq, (q + 1) * kq)
        value = means_ref[:, at]
        for dy in range(1, ny):
            second[dy, q].wait_recv()
            arrived, slot = incoming(q)
            value = value + arrived[dy - 1, slot].astype(jnp.float32)
        means_ref[:, at] = value / mass[:, at]

    for copy in pending:
        copy.wait_send()


def solution(mesh):
    nc, nd = mesh.shape["cent"], mesh.shape["dp"]
    ny = nd // 2
    nx = ny if nc % ny == 0 else 1
    nq = 8
    narrow = nq // 4

    def per_device(features, centroids, row_weight, centroid_share):
        rows, dloc = features.shape
        kc, width = centroids.shape
        ds = width // nd
        f32, bf16 = jnp.float32, jnp.bfloat16
        dma = pltpu.SemaphoreType.DMA
        vmem = pl.BlockSpec(memory_space=pltpu.VMEM)
        means, mass = pl.pallas_call(
            functools.partial(kernel_body, nc, nd, nx, nq),
            out_shape=(
                jax.ShapeDtypeStruct((ds, kc), f32),
                jax.ShapeDtypeStruct((1, kc), f32),
            ),
            in_specs=[vmem, pl.BlockSpec(memory_space=pl.ANY), vmem, vmem],
            out_specs=(vmem, vmem),
            scratch_shapes=[
                pltpu.VMEM((kc, width), bf16),
                dma(()),
                pltpu.VMEM((width, rows), bf16),
                pltpu.VMEM((kc, rows), f32),
                pltpu.VMEM((kc, rows), bf16),
                pltpu.VMEM((2, rows), f32),
                pltpu.VMEM((nc, 2, rows), f32),
                pltpu.VMEM((ITERS, 1, rows), f32),
                pltpu.VMEM((ITERS, nc, 1, rows), f32),
                pltpu.VMEM((ITERS + 1, 1, kc), f32),
                pltpu.VMEM((ITERS + 1, nd, 1, kc), f32),
                pltpu.VMEM((ny, nq, ds, kc // nq), f32),
                pltpu.VMEM((ny, nq, ds, kc // nq), f32),
                pltpu.VMEM((ny - 1, nq - narrow, ds, kc // nq), f32),
                pltpu.VMEM((ny - 1, nq - narrow, ds, kc // nq), f32),
                pltpu.VMEM((ny - 1, narrow, ds, kc // nq), bf16),
                pltpu.VMEM((ny - 1, narrow, ds, kc // nq), bf16),
                dma((nc, 2)), dma((nc, 2)),
                dma((nc,)), dma((nc,)),
                dma((ITERS, nc)), dma((ITERS, nc)),
                dma((ITERS + 1, nd)), dma((ITERS + 1, nd)),
                dma((ny, nq)), dma((ny, nq)),
                dma((ny - 1, nq)), dma((ny - 1, nq)),
            ],
            compiler_params=pltpu.CompilerParams(
                collective_id=0, has_side_effects=True, vmem_limit_bytes=50 * 1024 * 1024
            ),
        )(features.T, centroids, row_weight[None], centroid_share[None])
        return means, mass[0]

    in_specs = (P("dp", "cent"), P("cent", None), P("dp"), P("cent"))
    out_specs = (P("dp", "cent"), P("cent"))
    return jax.shard_map(
        per_device, mesh=mesh, in_specs=in_specs, out_specs=out_specs, check_vma=False
    )
```
